1024 devices in a mesh: section: 4 (over y_hi), ctx: 32 (over z, y_lo), tp: 8 (over x, core).
Axes of the slice: x: 4, y: 8 (y_hi: 4, y_lo: 2; y = y_hi * 2 + y_lo), z: 16, core: 2. Of those that a mesh axis runs over, the one named last changes fastest.
Arguments:
- mamba_input: bfloat16 [4, 4096, 8192], P('section', 'ctx', 'tp'), may hold values from -6 to 6
- mamba_gate: bfloat16 [4, 4096, 8192], P('section', 'ctx', 'tp'), may hold values from -6 to 6
- write_vectors: bfloat16 [4, 4096, 1024], P('section', 'ctx', 'tp'), may hold values from -0.546875 to 0.546875
- read_vectors: bfloat16 [4, 4096, 1024], P('section', 'ctx', 'tp'), may hold values from -6 to 6
- step_sizes: float32 [4, 128, 4096], P('section', 'tp', 'ctx'), may hold values from 0.05 to 0.5
- decay_rates: float32 [4, 128], P('section', 'tp'), may hold values from 0.0002 to 0.3
- skip_scale: float32 [4, 128], P('section', 'tp'), may hold values from 0.5 to 1.5
- norm_gain: float32 [4, 8192], P('section', 'tp'), may hold values from 0.5 to 1.5
- attn_queries: bfloat16 [4, 4096, 4096], P('section', 'ctx', 'tp'), may hold values from -180 to 180
- attn_keys: bfloat16 [4, 4096, 1024], P('section', 'ctx', 'tp'), may hold values from -8 to 8
- attn_values: bfloat16 [4, 4096, 1024], P('section', 'ctx', 'tp'), may hold values from -6 to 6
- block_order: int32 [4, 64], P('section'), may hold values from 0 to 63, each once within a row
Outputs:
- handed: bfloat16 [4, 4096, 8192], P('section', 'ctx', 'tp')
- attended: bfloat16 [4, 4096, 4096], P('section', 'ctx', 'tp')
The draws below stay inside these ranges and needn't reach their ends.
Inputs may be any that keep to these rules, and one draw needn't show every extreme that they name: Each row of block_order names every half-block 0 to 63 once.
All inputs are finite; a program needn't handle non-finite values.
Results may differ from the reference program's by a relative error of at most 0.0095.
Values may be sent and summed in bfloat16 or wider, within the bound.
A program may use at most 64 MiB of HBM per device.

```python
import math
import jax
import jax.numpy as jnp
from jax import lax

TOK_DEV = 128
SPAN = 128
MHEADS = 128
HEADP = 64
NSTATE = 128
GROUPS = 8
AHEADS = 32
KVHEADS = 8
HEADD = 128
SECTIONS = 4
TOKENS = 4096
HALF = 64
MW = 8192
QW = 4096
KW = 1024
N_CTX = 32


def draw_decay_rates(key, part):
    spread = jax.random.uniform(jax.random.fold_in(key, 1), (SECTIONS, MHEADS), jnp.float32)
    picker = jax.random.uniform(jax.random.fold_in(key, 2), (SECTIONS, MHEADS), jnp.float32)
    share = 0.5
    fast = jnp.exp(jnp.log(0.1) + spread * jnp.log(3.0))
    slow = jnp.exp(jnp.log(0.0002) + spread * jnp.log(10.0))
    return jnp.where(picker < share, fast, slow).astype(jnp.float32)


def query_key_pair(key):
    queries = jnp.clip(jax.random.normal(jax.random.fold_in(key, 11), (SECTIONS, TOKENS, QW), jnp.float32), -6.0, 6.0)
    keys_out = jnp.clip(jax.random.normal(jax.random.fold_in(key, 12), (SECTIONS, TOKENS, KW), jnp.float32), -6.0, 6.0)
    return (queries, keys_out)


def draw_attn_queries(key, part):
    return query_key_pair(key)[0].astype(jnp.bfloat16)


def draw_attn_keys(key, part):
    return query_key_pair(key)[1].astype(jnp.bfloat16)


def level_of(own_key, extent, split, smallest, largest):
    factor_of = 1.0
    for position, shards_of in split:
        heights = jax.random.uniform(jax.random.fold_in(jax.random.fold_in(own_key, 6), position), (shards_of,), jnp.float32, smallest / len(split), largest / len(split))
        factor_of = factor_of * jnp.repeat(jnp.exp(heights), extent[position] // shards_of).reshape((-1,) + (1,) * (len(extent) - 1 - position))
    return factor_of


def normal_values(stream_key, dims, width, limit, shards=(), held_as=jnp.bfloat16):
    array = width * jax.random.normal(stream_key, dims, jnp.float32)
    if shards:
        array = array * level_of(stream_key, dims, shards, -0.22, 0.18)
    return jnp.clip(array, -limit, limit).astype(held_as)


def setup_inputs(seed: int = 0) -> dict:
    arg_keys = jax.random.split(jax.random.key(seed), 13)
    return {
        "mamba_input": normal_values(arg_keys[0], (SECTIONS, TOKENS, MW), 1.0, 6.0, ((0, 4), (1, 32), (2, 8))),
        "mamba_gate": normal_values(arg_keys[1], (SECTIONS, TOKENS, MW), 1.0, 6.0, ((0, 4), (1, 32), (2, 8))),
        "write_vectors": normal_values(arg_keys[2], (SECTIONS, TOKENS, GROUPS * NSTATE), 0.0884, 0.546875, ((0, 4), (1, 32), (2, 8))),
        "read_vectors": normal_values(arg_keys[3], (SECTIONS, TOKENS, GROUPS * NSTATE), 1.0, 6.0, ((0, 4), (1, 32), (2, 8))),
        "step_sizes": jnp.clip(jnp.exp(math.log(0.5) - 2.3025851 * jax.random.uniform(arg_keys[4], (SECTIONS, MHEADS, TOKENS), jnp.float32) ** level_of(arg_keys[4], (SECTIONS, MHEADS, TOKENS), ((0, 4), (1, 8), (2, 32)), -0.2, 0.2)), 0.05, 0.5),
        "decay_rates": draw_decay_rates(jax.random.fold_in(arg_keys[12], 71), 0),
        "skip_scale": jnp.clip(0.5 + 1.0 * jax.random.uniform(arg_keys[6], (SECTIONS, MHEADS), jnp.float32) ** level_of(arg_keys[6], (SECTIONS, MHEADS), ((0, 4), (1, 8)), -0.2, 0.2), 0.5, 1.5),
        "norm_gain": jnp.clip(1.0 + 0.1 * jax.random.normal(arg_keys[7], (SECTIONS, MW), jnp.float32), 0.5, 1.5),
        "attn_queries": draw_attn_queries(jax.random.fold_in(arg_keys[12], 71), 0),
        "attn_keys": draw_attn_keys(jax.random.fold_in(arg_keys[12], 71), 0),
        "attn_values": normal_values(arg_keys[10], (SECTIONS, TOKENS, KW), 1.0, 6.0, ((0, 4), (1, 32), (2, 8))),
        "block_order": jax.vmap(lambda own: jax.random.permutation(own, 2 * N_CTX))(jax.random.split(arg_keys[11], SECTIONS)).reshape((SECTIONS, 2 * N_CTX)).astype(jnp.int32),
    }


def mamba_section(inputs, gates, writes, reads, steps_in, rates, skips, gains):
    per_group = MHEADS // GROUPS
    span_count = TOKENS // SPAN
    x_spans = inputs.reshape(span_count, SPAN, MHEADS, HEADP)
    write_heads = jnp.repeat(writes.reshape(span_count, SPAN, GROUPS, NSTATE), per_group, axis=2)
    read_heads = jnp.repeat(reads.reshape(span_count, SPAN, GROUPS, NSTATE), per_group, axis=2)
    step_spans = steps_in.reshape(MHEADS, span_count, SPAN).transpose(1, 0, 2)
    lower = jnp.tril(jnp.ones((SPAN, SPAN), dtype=bool))

    def advance(state, items):
        x_span, write_span, read_span, step_span = items
        x_float = x_span.astype(jnp.float32)
        read_float = read_span.astype(jnp.float32)
        write_float = write_span.astype(jnp.float32)
        log_decay = jnp.cumsum(-rates[:, None] * step_span, axis=1)
        intersections = jnp.einsum('thn,shn->hts', read_float, write_float)
        spread = log_decay[:, :, None] - log_decay[:, None, :]
        decay_pairs = jnp.exp(jnp.where(lower[None], spread, 0.0))
        mixing = jnp.where(lower[None], intersections * decay_pairs * step_span[:, None, :], 0.0)
        mixing = lax.optimization_barrier(mixing.astype(jnp.bfloat16)).astype(jnp.float32)
        inner = jnp.einsum('hts,shp->thp', mixing, x_float)
        carried = jnp.einsum('thn,hpn->thp', read_float, state, precision=lax.Precision.HIGHEST)
        carried = carried * jnp.exp(log_decay).T[:, :, None]
        output = inner + carried + skips[None, :, None] * x_float
        to_end = step_span * jnp.exp(log_decay[:, -1:] - log_decay)
        weighted = (x_float * to_end.T[:, :, None]).astype(jnp.bfloat16)
        weighted = lax.optimization_barrier(weighted).astype(jnp.float32)
        contrib = jnp.einsum('shp,shn->hpn', weighted, write_float)
        state = jnp.exp(log_decay[:, -1])[:, None, None] * state + contrib
        return (state, output)
    start_state = jnp.zeros((MHEADS, HEADP, NSTATE), jnp.float32)
    outputs = lax.scan(advance, start_state, (x_spans, write_heads, read_heads, step_spans))[1]
    outputs = outputs.reshape(TOKENS, MHEADS, HEADP)
    gated = outputs * jax.nn.silu(gates.reshape(TOKENS, MHEADS, HEADP).astype(jnp.float32))
    grouped = gated.reshape(TOKENS, GROUPS, per_group * HEADP)
    factor = lax.rsqrt(lax.optimization_barrier(jnp.mean(grouped * grouped, axis=-1, keepdims=True)) + 1e-05)
    normed = grouped * factor * gains.reshape(GROUPS, per_group * HEADP)[None]
    return normed.astype(jnp.bfloat16).reshape(TOKENS, MW)

def attend_section(queries, keys_in, values_in, order):
    per_kv = AHEADS // KVHEADS
    row_index = jnp.arange(TOKENS, dtype=jnp.int32)
    positions = order[row_index // HALF] * HALF + row_index % HALF
    query_heads = queries.reshape(TOKENS, KVHEADS, per_kv, HEADD).transpose(1, 0, 2, 3)
    key_heads = keys_in.reshape(TOKENS, KVHEADS, HEADD).transpose(1, 0, 2)
    value_heads = values_in.reshape(TOKENS, KVHEADS, HEADD).transpose(1, 0, 2)
    scale = 1.0 / jnp.sqrt(jnp.float32(HEADD))

    def one_head(items):
        query_group, key_group, value_group = items
        key_float = key_group.astype(jnp.float32)
        value_float = value_group.astype(jnp.float32)
        query_blocks = query_group.reshape(TOKENS // TOK_DEV, TOK_DEV, per_kv, HEADD)
        block_positions = positions.reshape(TOKENS // TOK_DEV, TOK_DEV)

        def one_block(pair):
            query_block, query_pos = pair
            scores = jnp.einsum('tqd,kd->qtk', query_block.astype(jnp.float32), key_float) * scale
            visible = positions[None, None, :] <= query_pos[None, :, None]
            peak = lax.optimization_barrier(jnp.max(jnp.where(visible, scores, -jnp.inf), axis=2, keepdims=True))
            weights = jnp.where(visible, jnp.exp(scores - peak), 0.0)
            total = lax.optimization_barrier(jnp.sum(weights, axis=2, keepdims=True))
            rounded = lax.optimization_barrier(weights.astype(jnp.bfloat16)).astype(jnp.float32)
            result = jnp.einsum('qtk,kd->qtd', rounded, value_float) / total
            return result.transpose(1, 0, 2)
        return lax.map(one_block, (query_blocks, block_positions)).reshape(TOKENS, per_kv, HEADD)
    result = lax.map(one_head, (query_heads, key_heads, value_heads))
    return result.transpose(1, 0, 2, 3).reshape(TOKENS, QW).astype(jnp.bfloat16)

def reference(mamba_input, mamba_gate, write_vectors, read_vectors, step_sizes, decay_rates, skip_scale, norm_gain, attn_queries, attn_keys, attn_values, block_order):
    mixed_all = []
    attended_all = []
    for section_idx in range(SECTIONS):
        mixed_all.append(mamba_section(mamba_input[section_idx], mamba_gate[section_idx], write_vectors[section_idx], read_vectors[section_idx], step_sizes[section_idx], decay_rates[section_idx], skip_scale[section_idx], norm_gain[section_idx]))
        attended_all.append(attend_section(attn_queries[section_idx], attn_keys[section_idx], attn_values[section_idx], block_order[section_idx]))
    handed = jnp.roll(jnp.stack(mixed_all), 1, axis=0)
    return (handed, jnp.stack(attended_all))
```

```python
import functools
import math

import jax
import jax.numpy as jnp
from jax import lax
from jax.experimental import pallas as pl
from jax.experimental.pallas import tpu as pltpu
from jax.sharding import PartitionSpec as P

MESH = pl.DeviceIdType.MESH
F32 = jnp.float32
BF16 = jnp.bfloat16
HIGH = lax.Precision.HIGHEST
NEG = -1e30
TOK = 128
HALF = 64
HEADS = 16
HEADP = 64
FEAT = HEADS * HEADP
TILES = FEAT // 128
OWN = TILES // 2
QH = 4
SCALE2 = math.log2(math.e) / math.sqrt(128.0)


def contract(a, b, da, db, precision=None):
    return lax.dot_general(
        a, b, (((da,), (db,)), ((), ())), precision=precision, preferred_element_type=F32
    )


def kernel(
    nz,
    nsec,
    x_ref,
    gate_ref,
    b_ref,
    c_ref,
    step_ref,
    rate_ref,
    skip_ref,
    gain_ref,
    q_ref,
    k_ref,
    v_ref,
    order_ref,
    hand_ref,
    att_ref,
    kv,
    qall,
    peak,
    den,
    acc,
    ecum,
    rhs,
    lhs,
    drow,
    ctile,
    crecv,
    drecv,
    dpair,
    pbuf,
    arecv,
    adec,
    pref,
    sin,
    ssend,
    gated,
    mixed,
    osend,
    orecv,
    stsend,
    strecv,
    kv_ss,
    kv_rs,
    y_ss,
    y_rs,
    a_ss,
    a_rs,
    ad_ss,
    ad_rs,
    r_ss,
    r_rs,
    h_ss,
    h_rs,
):
    sec = lax.axis_index("section")
    ctx = lax.axis_index("ctx")
    z = ctx // 2
    y = ctx % 2
    half = nz // 2
    rows = OWN * TOK // nz
    partner = {"ctx": z * 2 + 1 - y}

    def at_z(k):
        return {"ctx": k * 2 + y}

    def around(k):
        return lax.rem(k + nz, nz)

    following = {"section": lax.rem(sec + 1, nsec)}
    previous = {"section": lax.rem(sec + nsec - 1, nsec)}

    def copy(src, dst, ss, rs, to):
        return pltpu.make_async_remote_copy(
            src_ref=src, dst_ref=dst, send_sem=ss, recv_sem=rs, device_id=to, device_id_type=MESH
        )

    sent = []

    def start(c):
        c.start()
        sent.append(c)

    barrier = pltpu.get_barrier_semaphore()
    for o in range(1, nz):
        pl.semaphore_signal(barrier, inc=1, device_id=at_z(around(z + o)), device_id_type=MESH)
    for to in (partner, following, previous):
        pl.semaphore_signal(barrier, inc=1, device_id=to, device_id_type=MESH)

    kv[z, 0] = k_ref[...]
    kv[z, 1] = v_ref[...]
    for h in range(QH):
        qall[h * TOK : (h + 1) * TOK] = q_ref[:, h * 128 : (h + 1) * 128]
    pl.semaphore_wait(barrier, nz - 1 + 3)

    def ring_copy(way, s, t, arriving):
        if way == 0:
            slot, to = (around(z - s), z) if arriving else (around(z - s + 1), around(z + 1))
        else:
            slot, to = (around(z + s), z) if arriving else (around(z + s - 1), around(z - 1))
        if arriving:
            to = around(z + 1)
        place = kv.at[slot, t]
        return copy(place, place, kv_ss.at[way, s, t], kv_rs.at[way, s, t], at_z(to))

    def ring_parts(s):
        if s < half:
            return [(w, t) for t in (0, 1) for w in (0, 1)]
        return [(0, 0), (1, 1)]

    def ring_send(s):
        for w, t in ring_parts(s):
            start(ring_copy(w, s, t, False))

    def ring_hop(s):
        going = ring_parts(s + 1) if s < half else []
        for w, t in ring_parts(s):
            ring_copy(w, s, t, True).wait_recv()
            if (w, t) in going:
                start(ring_copy(w, s + 1, t, False))

    ring_send(1)
    start(copy(qall.at[pl.ds(0, QH * TOK)], qall.at[pl.ds(QH * TOK, QH * TOK)], y_ss.at[0], y_rs.at[0], partner))

    row16 = lax.broadcasted_iota(jnp.int32, (HEADS, TOK), 0)
    rate = jnp.zeros((HEADS, TOK), F32)
    for h in range(HEADS):
        rate = jnp.where(row16 == h, rate_ref[0, h], rate)
    row = lax.broadcasted_iota(jnp.int32, (TOK, 128), 0)
    lane = lax.broadcasted_iota(jnp.int32, (TOK, 128), 1)
    step = step_ref[...]
    upper = jnp.where(row <= lane, 1.0, 0.0).astype(F32)
    cum = contract(-rate * step, upper, 1, 0, HIGH)
    scales = jnp.concatenate([jnp.exp(cum), jnp.exp(-cum) * step], axis=1)
    head_of = lax.shift_right_logical(lax.broadcasted_iota(jnp.int32, (HEADS, FEAT), 1), 6)
    spread = jnp.where(head_of == lax.broadcasted_iota(jnp.int32, (HEADS, FEAT), 0), 1.0, 0.0)
    for j in range(TILES):
        cols = slice(j * 128, (j + 1) * 128)
        wide = contract(scales, spread[:, cols], 0, 0, HIGH)
        ecum[:, cols] = wide[:TOK]
        drow[j] = wide[TOK - 1 : TOK]
        xf = (x_ref[:, cols].astype(F32) * wide[TOK:]).astype(BF16)
        rhs[j, 0:TOK] = xf
        ctile[j] = (contract(b_ref[...], xf, 0, 0) * wide[TOK - 1 : TOK]).astype(BF16)
    theirs = (1 - y) * OWN
    mine = y * OWN
    start(copy(drow.at[pl.ds(theirs, OWN)], drecv, y_ss.at[1], y_rs.at[1], partner))
    for c in range(OWN):
        start(copy(ctile.at[theirs + c], crecv.at[c], y_ss.at[2 + c], y_rs.at[2 + c], partner))
    inner = contract(c_ref[...], b_ref[...], 1, 1)
    lhs[:, 0:TOK] = jnp.where(lane <= row, inner, 0.0).astype(BF16)
    lhs[:, TOK:] = c_ref[...]

    row_in = jnp.bitwise_and(row, HALF - 1)
    lane1 = lax.broadcasted_iota(jnp.int32, (1, 128), 1)

    def query_pos(at):
        o0 = order_ref[0, 2 * at]
        o1 = order_ref[0, 2 * at + 1]
        return jnp.where(lane1 < HALF, o0, o1) * HALF + jnp.bitwise_and(lane1, HALF - 1)

    qpos = [query_pos(ctx), query_pos(z * 2 + 1 - y)]
    peak[...] = jnp.full(peak.shape, NEG, F32)
    den[...] = jnp.zeros(den.shape, F32)
    acc[...] = jnp.zeros(acc.shape, F32)

    def attend(slots):
        biases = []
        for slot in slots:
            at = slot * 2 + y
            o0 = order_ref[0, 2 * at]
            o1 = order_ref[0, 2 * at + 1]
            kpos = jnp.where(row < HALF, o0, o1) * HALF + row_in
            biases.append([jnp.where(kpos <= p, 0.0, NEG).astype(F32) for p in qpos])
        keys = jnp.concatenate([kv[s, 0] for s in slots], axis=0)
        values = jnp.concatenate([kv[s, 1] for s in slots], axis=0)
        for src in range(2):
            bias = jnp.concatenate([b[src] for b in biases], axis=0)
            bias = jnp.concatenate([bias, bias], axis=1)
            for pair in range(QH // 2):
                cols = slice(src * QH * TOK + pair * 256, src * QH * TOK + (pair + 1) * 256)
                scores = contract(keys, qall[cols], 1, 1) + bias
                old = peak[:, cols]
                new = jnp.maximum(old, jnp.max(scores, axis=0, keepdims=True))
                weights = jnp.exp2((scores - new) * SCALE2)
                fade = jnp.exp2((old - new) * SCALE2)
                peak[:, cols] = new
                den[:, cols] = den[:, cols] * fade + jnp.sum(weights, axis=0, keepdims=True)
                acc[:, cols] = acc[:, cols] * fade + contract(values, weights.astype(BF16), 0, 0)

    def attend_step(s):
        if s < half:
            attend([around(z - s), around(z + s)])
        else:
            attend([around(z - s)])

    hops = iter(range(1, half + 1))
    steps = iter(range(1, half + 1))

    def hop(n):
        for _ in range(n):
            s = next(hops, None)
            if s is not None:
                ring_hop(s)

    def work(n):
        for _ in range(n):
            s = next(steps, None)
            if s is not None:
                attend_step(s)

    copy(qall.at[pl.ds(0, QH * TOK)], qall.at[pl.ds(QH * TOK, QH * TOK)], y_ss.at[0], y_rs.at[0], partner).wait_recv()
    hop(1)
    attend([z])

    yf = y.astype(F32)
    copy(drow.at[pl.ds(theirs, OWN)], drecv, y_ss.at[1], y_rs.at[1], partner).wait_recv()
    for c in range(OWN):
        copy(ctile.at[theirs + c], crecv.at[c], y_ss.at[2 + c], y_rs.at[2 + c], partner).wait_recv()
        d_mine = drow[mine + c]
        d_other = drecv[c]
        dpair[c] = d_mine * d_other
        a = d_other * (1.0 - yf) + yf
        b = d_mine * yf + (1.0 - yf)
        total = ctile[mine + c].astype(F32) * a + crecv[c].astype(F32) * b
        for r in range(TOK // rows):
            pbuf[c * (TOK // rows) + r] = total[r * rows : (r + 1) * rows].astype(BF16)
    per_tile = TOK // rows
    far_first = sorted(range(1, nz), key=lambda o: -min(o, nz - o))
    for o in far_first:
        k = around(z + o)
        start(copy(dpair.at[k // per_tile], adec.at[z], ad_ss.at[o], ad_rs.at[z], at_z(k)))
        start(copy(pbuf.at[k], arecv.at[z], a_ss.at[o], a_rs.at[z], at_z(k)))
    arecv[z] = pbuf[z]
    adec[z] = dpair[z // per_tile]

    hop(1)
    work(1)
    hop(1)
    work(1)

    for o in range(1, nz):
        k = around(z + o)
        copy(dpair.at[0], adec.at[k], ad_ss.at[o], ad_rs.at[k], at_z(k)).wait_recv()
        copy(pbuf.at[k], arecv.at[k], a_ss.at[o], a_rs.at[k], at_z(k)).wait_recv()
    state = jnp.zeros((rows, 128), F32)
    for k in range(nz):
        pref[k] = state.astype(BF16)
        state = adec[k] * state + arecv[k].astype(F32)
    for o in far_first:
        k = around(z + o)
        start(copy(pref.at[k], sin.at[z], r_ss.at[o], r_rs.at[z], at_z(k)))
    sin[z] = pref[z]

    hop(1)
    work(1)
    hop(1)
    work(1)

    for o in range(1, nz):
        k = around(z + o)
        copy(pref.at[k], sin.at[k], r_ss.at[o], r_rs.at[k], at_z(k)).wait_recv()
    for c in range(OWN):
        first = jnp.concatenate([sin[c * per_tile + r] for r in range(per_tile)], axis=0).astype(F32)
        d_mine = drow[mine + c]
        d_other = drecv[c]
        d0 = d_mine * (1.0 - yf) + d_other * yf
        c0 = ctile[mine + c].astype(F32) * (1.0 - yf) + crecv[c].astype(F32) * yf
        second = d0 * first + c0
        ssend[c] = (second * (1.0 - yf) + first * yf).astype(BF16)
        place = rhs.at[mine + c, pl.ds(TOK, 128)]
        start(copy(ssend.at[c], place, y_ss.at[2 + OWN + c], y_rs.at[2 + OWN + c], partner))
        rhs[mine + c, TOK:] = (first * (1.0 - yf) + second * yf).astype(BF16)

    hop(1)
    work(1)
    hop(1)
    work(1)

    for c in range(OWN):
        place = rhs.at[theirs + c, pl.ds(TOK, 128)]
        copy(ssend.at[c], place, y_ss.at[2 + OWN + c], y_rs.at[2 + OWN + c], partner).wait_recv()
    squares = jnp.zeros((TOK, 128), F32)
    for j in range(TILES):
        cols = slice(j * 128, (j + 1) * 128)
        skip = jnp.where(lane1 < HEADP, skip_ref[0, 2 * j], skip_ref[0, 2 * j + 1])
        out = ecum[:, cols] * contract(lhs[...], rhs[j], 1, 0) + skip * x_ref[:, cols].astype(F32)
        gate = gate_ref[:, cols].astype(F32)
        value = out * (gate / (1.0 + jnp.exp(-gate)))
        gated[:, cols] = value
        squares += value * value
    factor = lax.rsqrt(jnp.sum(squares, axis=1, keepdims=True) * (1.0 / FEAT) + 1e-5)
    parts = 4
    span = TOK // parts
    for p in range(parts):
        at = slice(p * span, (p + 1) * span)
        mixed[at] = (gated[at] * factor[at] * gain_ref[...]).astype(BF16)
        place = pl.ds(p * span, span)
        start(copy(mixed.at[place], hand_ref.at[place], h_ss.at[p], h_rs.at[p], following))

    hop(half)
    work(half)

    mine_cols = slice(0, QH * TOK)
    other_cols = slice(QH * TOK, 2 * QH * TOK)
    osend[...] = (acc[:, other_cols] / den[:, other_cols]).astype(BF16)
    stsend[0] = peak[:, other_cols]
    stsend[1] = den[:, other_cols]
    swap = copy(osend, orecv, y_ss.at[2 + 2 * OWN], y_rs.at[2 + 2 * OWN], partner)
    swap_stats = copy(stsend, strecv, y_ss.at[3 + 2 * OWN], y_rs.at[3 + 2 * OWN], partner)
    start(swap_stats)
    start(swap)
    swap_stats.wait_recv()
    swap.wait_recv()
    m1 = peak[:, mine_cols]
    m2 = strecv[0]
    top = jnp.maximum(m1, m2)
    w1 = jnp.exp2((m1 - top) * SCALE2)
    w2 = jnp.exp2((m2 - top) * SCALE2) * strecv[1]
    inv = 1.0 / (w1 * den[:, mine_cols] + w2)
    w1 = w1 * inv
    w2 = w2 * inv
    for h in range(QH):
        cols = slice(h * TOK, (h + 1) * TOK)
        both = acc[:, cols] * w1[:, cols] + orecv[:, cols].astype(F32) * w2[:, cols]
        att_ref[:, cols] = both.T.astype(BF16)

    for p in range(parts):
        place = pl.ds(p * span, span)
        copy(mixed.at[place], hand_ref.at[place], h_ss.at[p], h_rs.at[p], following).wait_recv()
    for c in sent:
        c.wait_send()


def shards(nz, nsec, *args):
    flat = [a.reshape(a.shape[1:]) if a.ndim == 3 else a for a in args]
    rows = OWN * TOK // nz
    half = nz // 2
    vmem = pl.BlockSpec(memory_space=pltpu.VMEM)
    smem = pl.BlockSpec(memory_space=pltpu.SMEM)
    in_specs = [vmem] * 5 + [smem, smem] + [vmem] * 4 + [smem]
    dma = pltpu.SemaphoreType.DMA
    swaps = 4 + 2 * OWN
    handed, attended = pl.pallas_call(
        functools.partial(kernel, nz, nsec),
        out_shape=(
            jax.ShapeDtypeStruct((TOK, FEAT), BF16),
            jax.ShapeDtypeStruct((TOK, QH * 128), BF16),
        ),
        in_specs=in_specs,
        out_specs=(vmem, vmem),
        scratch_shapes=[
            pltpu.VMEM((nz, 2, TOK, 128), BF16),
            pltpu.VMEM((2 * QH * TOK, 128), BF16),
            pltpu.VMEM((1, 2 * QH * TOK), F32),
            pltpu.VMEM((1, 2 * QH * TOK), F32),
            pltpu.VMEM((128, 2 * QH * TOK), F32),
            pltpu.VMEM((TOK, FEAT), F32),
            pltpu.VMEM((TILES, TOK + 128, 128), BF16),
            pltpu.VMEM((TOK, TOK + 128), BF16),
            pltpu.VMEM((TILES, 1, 128), F32),
            pltpu.VMEM((TILES, 128, 128), BF16),
            pltpu.VMEM((OWN, 128, 128), BF16),
            pltpu.VMEM((OWN, 1, 128), F32),
            pltpu.VMEM((OWN, 1, 128), F32),
            pltpu.VMEM((nz, rows, 128), BF16),
            pltpu.VMEM((nz, rows, 128), BF16),
            pltpu.VMEM((nz, 1, 128), F32),
            pltpu.VMEM((nz, rows, 128), BF16),
            pltpu.VMEM((nz, rows, 128), BF16),
            pltpu.VMEM((OWN, 128, 128), BF16),
            pltpu.VMEM((TOK, FEAT), F32),
            pltpu.VMEM((TOK, FEAT), BF16),
            pltpu.VMEM((128, QH * TOK), BF16),
            pltpu.VMEM((128, QH * TOK), BF16),
            pltpu.VMEM((2, 1, QH * TOK), F32),
            pltpu.VMEM((2, 1, QH * TOK), F32),
            dma((2, half + 1, 2)),
            dma((2, half + 1, 2)),
            dma((swaps,)),
            dma((swaps,)),
            dma((nz,)),
            dma((nz,)),
            dma((nz,)),
            dma((nz,)),
            dma((nz,)),
            dma((nz,)),
            dma((4,)),
            dma((4,)),
        ],
        compiler_params=pltpu.CompilerParams(
            collective_id=0, has_side_effects=True, vmem_limit_bytes=32 * 1024 * 1024
        ),
        cost_estimate=pl.CostEstimate(
            flops=1300000000, bytes_accessed=1400000, transcendentals=2500000
        ),
    )(*flat)
    return handed[None], attended[None]


def solution(mesh):
    nz = mesh.shape["ctx"] // 2
    nsec = mesh.shape["section"]
    wide = P("section", "ctx", "tp")
    return jax.shard_map(
        functools.partial(shards, nz, nsec),
        mesh=mesh,
        in_specs=(
            wide,
            wide,
            wide,
            wide,
            P("section", "tp", "ctx"),
            P("section", "tp"),
            P("section", "tp"),
            P("section", "tp"),
            wide,
            wide,
            wide,
            P("section", None),
        ),
        out_specs=(wide, wide),
        check_vma=False,
    )
```

```python
import functools
import math

import jax
import jax.numpy as jnp
from jax import lax
from jax.experimental import pallas as pl
from jax.experimental.pallas import tpu as pltpu
from jax.sharding import PartitionSpec as P

MESH = pl.DeviceIdType.MESH
F32 = jnp.float32
BF16 = jnp.bfloat16
HIGH = lax.Precision.HIGHEST
NEG = -1e30
TOK = 128
HALF = 64
HEADS = 16
HEADP = 64
FEAT = HEADS * HEADP
TILES = FEAT // 128
OWN = TILES // 2
QH = 4
SCALE2 = math.log2(math.e) / math.sqrt(128.0)


def contract(a, b, da, db, precision=None):
    return lax.dot_general(
        a, b, (((da,), (db,)), ((), ())), precision=precision, preferred_element_type=F32
    )


def kernel(
    nz,
    nsec,
    x_in,
    gate_in,
    b_in,
    c_in,
    step_in,
    rate_in,
    skip_in,
    gain_in,
    q_in,
    k_in,
    v_in,
    order_in,
    hand_ref,
    att_ref,
    xs,
    gates,
    writes,
    reads,
    steps,
    rate_ref,
    skip_ref,
    gain_ref,
    order_ref,
    kv,
    qall,
    peak,
    den,
    acc,
    ecum,
    rhs,
    lhs,
    drow,
    cstate,
    dpair,
    pbuf,
    arecv,
    adec,
    pref,
    sin,
    ubuf,
    hrecv,
    sqsend,
    sqrecv,
    osend,
    orecv,
    stsend,
    strecv,
    kv_ss,
    kv_rs,
    y_ss,
    y_rs,
    a_ss,
    a_rs,
    ad_ss,
    ad_rs,
    r_ss,
    r_rs,
    h_ss,
    h_rs,
    in_s,
):
    sec = lax.axis_index("section")
    ctx = lax.axis_index("ctx")
    z = ctx // 2
    y = ctx % 2
    half = nz // 2
    rows = OWN * TOK // nz
    per_tile = TOK // rows
    wide = OWN * 128
    partner = {"ctx": z * 2 + 1 - y}

    def at_z(k):
        return {"ctx": k * 2 + y}

    def around(k):
        return lax.rem(k + nz, nz)

    def in_section(i, t):
        return {"section": lax.rem(sec + i, nsec), "ctx": z * 2 + t}

    def copy(src, dst, ss, rs, to):
        return pltpu.make_async_remote_copy(
            src_ref=src, dst_ref=dst, send_sem=ss, recv_sem=rs, device_id=to, device_id_type=MESH
        )

    sent = []

    def start(c):
        c.start()
        sent.append(c)

    mine = pl.ds(pl.multiple_of(y * wide, 128), wide)

    def theirs(start_at, width):
        return pl.ds(pl.multiple_of((1 - y) * wide + start_at, 128), width)

    fetches = [
        (step_in, steps.at[y]),
        (rate_in, rate_ref),
        (x_in.at[:, mine], xs.at[y]),
        (b_in, writes.at[y]),
        (k_in, kv.at[z, 0]),
        (v_in, kv.at[z, 1]),
        (c_in, reads.at[y]),
        (q_in.at[:, 0:128], qall.at[0:TOK]),
        (q_in.at[:, 128:256], qall.at[TOK : 2 * TOK]),
        (q_in.at[:, 256:384], qall.at[2 * TOK : 3 * TOK]),
        (q_in.at[:, 384:512], qall.at[3 * TOK : 4 * TOK]),
        (order_in, order_ref),
        (gate_in.at[:, mine], gates.at[y]),
        (skip_in, skip_ref),
        (gain_in.at[:, mine], gain_ref),
    ]
    fetches = [pltpu.make_async_copy(s, d, in_s.at[i]) for i, (s, d) in enumerate(fetches)]

    barrier = pltpu.get_barrier_semaphore()
    for o in range(1, nz):
        pl.semaphore_signal(barrier, inc=1, device_id=at_z(around(z + o)), device_id_type=MESH)
    for to in (
        partner,
        in_section(1, 0),
        in_section(1, 1),
        in_section(nsec - 1, 0),
        in_section(nsec - 1, 1),
    ):
        pl.semaphore_signal(barrier, inc=1, device_id=to, device_id_type=MESH)
    for f in fetches:
        f.start()
    pl.semaphore_wait(barrier, nz - 1 + 5)

    hw = wide // 2
    give_steps = copy(step_in, steps.at[y], y_ss.at[0], y_rs.at[0], partner)
    give_b = copy(b_in, writes.at[y], y_ss.at[1], y_rs.at[1], partner)
    give_x = [
        copy(
            x_in.at[:, theirs(i * hw, hw)],
            xs.at[y, :, i * hw : (i + 1) * hw],
            y_ss.at[2 + i],
            y_rs.at[2 + i],
            partner,
        )
        for i in range(2)
    ]
    give_c = copy(c_in, reads.at[y], y_ss.at[4], y_rs.at[4], partner)
    give_gate = copy(gate_in.at[:, theirs(0, wide)], gates.at[y], y_ss.at[5], y_rs.at[5], partner)
    give_q = copy(
        qall.at[pl.ds(0, QH * TOK)], qall.at[pl.ds(QH * TOK, QH * TOK)], y_ss.at[6], y_rs.at[6], partner
    )
    for c in (give_steps, give_b, *give_x):
        start(c)

    def ring_copy(way, s, t, arriving):
        if way == 0:
            slot, to = around(z - s + (0 if arriving else 1)), around(z + 1)
        else:
            slot, to = around(z + s - (0 if arriving else 1)), around(z - 1)
        place = kv.at[slot, t]
        return copy(place, place, kv_ss.at[way, s, t], kv_rs.at[way, s, t], at_z(to))

    def ring_parts(s):
        if s < half:
            return [(w, t) for t in (0, 1) for w in (0, 1)]
        return [(0, 0), (1, 1)]

    def ring_hop(s):
        going = ring_parts(s + 1) if s < half else []
        for w, t in ring_parts(s):
            ring_copy(w, s, t, True).wait_recv()
            if (w, t) in going:
                start(ring_copy(w, s + 1, t, False))

    for f in fetches[:6]:
        f.wait()
    for w, t in ring_parts(1):
        start(ring_copy(w, 1, t, False))
    row16 = lax.broadcasted_iota(jnp.int32, (HEADS, TOK), 0)
    rate = jnp.zeros((HEADS, TOK), F32)
    for h in range(HEADS):
        rate = jnp.where(row16 == h, rate_ref[0, h], rate)
    row = lax.broadcasted_iota(jnp.int32, (TOK, 128), 0)
    lane = lax.broadcasted_iota(jnp.int32, (TOK, 128), 1)
    upper = jnp.where(row <= lane, 1.0, 0.0).astype(F32)
    lane_head = lax.shift_right_logical(lane[:HEADS], 6)

    def scales_of(t):
        step = steps[t]
        cum = contract(-rate * step, upper, 1, 0, HIGH)
        return jnp.concatenate([jnp.exp(cum), jnp.exp(-cum) * step], axis=1)

    def block_tile(t, scales, c):
        cols = slice(c * 128, (c + 1) * 128)
        spread = jnp.where(row16 - y * (2 * OWN) - 2 * c == lane_head, 1.0, 0.0).astype(F32)
        spread_out = contract(scales, spread, 0, 0, HIGH)
        ecum[t, c] = spread_out[:TOK]
        d = spread_out[TOK - 1 : TOK]
        drow[t, c] = d
        xf = (xs[t, :, cols].astype(F32) * spread_out[TOK:]).astype(BF16)
        rhs[t, c, 0:TOK] = xf
        cstate[t, c] = contract(writes[t], xf, 0, 0) * d

    def block_lhs(t):
        inner = contract(reads[t], writes[t], 1, 1)
        lhs[t, :, 0:TOK] = jnp.where(lane <= row, inner, 0.0).astype(BF16)
        lhs[t, :, TOK:] = reads[t]

    scales = scales_of(y)
    for c in range(OWN):
        block_tile(y, scales, c)
    for f in fetches[6:]:
        f.wait()
    start(give_c)
    start(give_q)
    start(give_gate)
    give_steps.wait_recv()
    give_b.wait_recv()
    scales = scales_of(1 - y)
    for c in range(OWN):
        if c % (OWN // 2) == 0:
            give_x[c // (OWN // 2)].wait_recv()
        block_tile(1 - y, scales, c)
        d1 = drow[1, c]
        dpair[c] = drow[0, c] * d1
        total = cstate[0, c] * d1 + cstate[1, c]
        for r in range(per_tile):
            pbuf[c * per_tile + r] = total[r * rows : (r + 1) * rows].astype(BF16)
    far_first = sorted(range(1, nz), key=lambda o: -min(o, nz - o))
    for o in far_first:
        k = around(z + o)
        start(copy(dpair.at[k // per_tile], adec.at[z], ad_ss.at[o], ad_rs.at[z], at_z(k)))
        start(copy(pbuf.at[k], arecv.at[z], a_ss.at[o], a_rs.at[z], at_z(k)))
    arecv[z] = pbuf[z]
    adec[z] = dpair[z // per_tile]

    row_in = jnp.bitwise_and(row, HALF - 1)
    lane1 = lax.broadcasted_iota(jnp.int32, (1, 128), 1)

    def query_pos(at):
        o0 = order_ref[0, 2 * at]
        o1 = order_ref[0, 2 * at + 1]
        return jnp.where(lane1 < HALF, o0, o1) * HALF + jnp.bitwise_and(lane1, HALF - 1)

    qpos = [query_pos(ctx), query_pos(z * 2 + 1 - y)]

    def attend(slots, first=False):
        biases = []
        for slot in slots:
            at = slot * 2 + y
            o0 = order_ref[0, 2 * at]
            o1 = order_ref[0, 2 * at + 1]
            kpos = jnp.where(row < HALF, o0, o1) * HALF + row_in
            biases.append([jnp.where(kpos <= p, 0.0, NEG).astype(F32) for p in qpos])
        keys = jnp.concatenate([kv[s, 0] for s in slots], axis=0)
        values = jnp.concatenate([kv[s, 1] for s in slots], axis=0)
        for src in range(2):
            bias = jnp.concatenate([b[src] for b in biases], axis=0)
            bias = jnp.concatenate([bias, bias], axis=1)
            for pair in range(QH // 2):
                cols = slice(src * QH * TOK + pair * 256, src * QH * TOK + (pair + 1) * 256)
                scores = contract(keys, qall[cols], 1, 1) + bias
                new = jnp.max(scores, axis=0, keepdims=True)
                if not first:
                    old = peak[:, cols]
                    new = jnp.maximum(old, new)
                weights = jnp.exp2((scores - new) * SCALE2)
                total = jnp.sum(weights, axis=0, keepdims=True)
                summed = contract(values, weights.astype(BF16), 0, 0)
                if not first:
                    fade = jnp.exp2((old - new) * SCALE2)
                    total += den[:, cols] * fade
                    summed += acc[:, cols] * fade
                peak[:, cols] = new
                den[:, cols] = total
                acc[:, cols] = summed

    def attend_step(s):
        if s < half:
            attend([around(z - s), around(z + s)])
        else:
            attend([around(z - s)])

    hops = iter(range(1, half + 1))
    parts = iter(range(1, half + 1))

    def hop():
        s = next(hops, None)
        if s is not None:
            ring_hop(s)

    def work():
        s = next(parts, None)
        if s is not None:
            attend_step(s)

    hop()
    give_c.wait_recv()
    block_lhs(0)
    block_lhs(1)
    give_q.wait_recv()
    hop()
    attend([z], first=True)
    work()

    for o in range(1, nz):
        k = around(z + o)
        copy(dpair.at[0], adec.at[k], ad_ss.at[o], ad_rs.at[k], at_z(k)).wait_recv()
        copy(pbuf.at[k], arecv.at[k], a_ss.at[o], a_rs.at[k], at_z(k)).wait_recv()
    state = jnp.zeros((rows, 128), F32)
    for k in range(nz):
        pref[k] = state.astype(BF16)
        state = adec[k] * state + arecv[k].astype(F32)
    for o in far_first:
        k = around(z + o)
        start(copy(pref.at[k], sin.at[z], r_ss.at[o], r_rs.at[z], at_z(k)))
    sin[z] = pref[z]

    hop()
    work()
    hop()
    work()
    give_gate.wait_recv()

    for o in range(1, nz):
        k = around(z + o)
        copy(pref.at[k], sin.at[k], r_ss.at[o], r_rs.at[k], at_z(k)).wait_recv()
    squares = [jnp.zeros((TOK, 128), F32) for _ in range(2)]
    for c in range(OWN):
        cols = slice(c * 128, (c + 1) * 128)
        enter = jnp.concatenate([sin[c * per_tile + r] for r in range(per_tile)], axis=0)
        rhs[0, c, TOK:] = enter
        rhs[1, c, TOK:] = (drow[0, c] * enter.astype(F32) + cstate[0, c]).astype(BF16)
        at = y * (2 * OWN) + 2 * c
        skip = jnp.where(lane1 < HEADP, skip_ref[0, at], skip_ref[0, at + 1])
        for t in range(2):
            out = ecum[t, c] * contract(lhs[t], rhs[t, c], 1, 0)
            out += skip * xs[t, :, cols].astype(F32)
            gate = gates[t, :, cols].astype(F32)
            value = out * (gate / (1.0 + jnp.exp(-gate)))
            squares[t] += value * value
            ubuf[t, c] = (value * gain_ref[:, cols]).astype(BF16)
            i = t * OWN + c
            start(copy(ubuf.at[t, c], hrecv.at[y, c], h_ss.at[i], h_rs.at[y, c], in_section(1, t)))
    ones = jnp.ones((8, 128), F32)
    for t in range(2):
        sqsend[t] = contract(ones, squares[t], 1, 1, HIGH)
        i = 2 * OWN + t
        start(copy(sqsend.at[t], sqrecv.at[y], h_ss.at[i], h_rs.at[y, OWN], in_section(1, t)))

    for _ in range(half):
        hop()
        work()

    mine_cols = slice(0, QH * TOK)
    other_cols = slice(QH * TOK, 2 * QH * TOK)
    osend[...] = (acc[:, other_cols] / den[:, other_cols]).astype(BF16)
    stsend[0] = peak[:, other_cols]
    stsend[1] = den[:, other_cols]
    swap = copy(osend, orecv, y_ss.at[7], y_rs.at[7], partner)
    swap_stats = copy(stsend, strecv, y_ss.at[8], y_rs.at[8], partner)
    start(swap_stats)
    start(swap)

    for u in range(2):
        for c in range(OWN):
            copy(ubuf.at[0, c], hrecv.at[u, c], h_ss.at[c], h_rs.at[u, c], partner).wait_recv()
        copy(sqsend.at[0], sqrecv.at[u], h_ss.at[2 * OWN], h_rs.at[u, OWN], partner).wait_recv()
    factor = lax.rsqrt((sqrecv[0] + sqrecv[1]) * (1.0 / FEAT) + 1e-5)
    pick = jnp.where(row[:8] == 0, 1.0, 0.0).astype(F32)
    factor = contract(factor, pick, 0, 0, HIGH)
    for u in range(2):
        for c in range(OWN):
            j = u * OWN + c
            hand_ref[:, j * 128 : (j + 1) * 128] = (hrecv[u, c].astype(F32) * factor).astype(BF16)

    swap_stats.wait_recv()
    swap.wait_recv()
    m1 = peak[:, mine_cols]
    m2 = strecv[0]
    top = jnp.maximum(m1, m2)
    w1 = jnp.exp2((m1 - top) * SCALE2)
    w2 = jnp.exp2((m2 - top) * SCALE2) * strecv[1]
    inv = 1.0 / (w1 * den[:, mine_cols] + w2)
    w1 = w1 * inv
    w2 = w2 * inv
    for h in range(QH):
        cols = slice(h * TOK, (h + 1) * TOK)
        both = acc[:, cols] * w1[:, cols] + orecv[:, cols].astype(F32) * w2[:, cols]
        att_ref[:, cols] = both.T.astype(BF16)

    for c in sent:
        c.wait_send()


def shards(nz, nsec, *args):
    flat = [a.reshape(a.shape[1:]) if a.ndim == 3 else a for a in args]
    rows = OWN * TOK // nz
    half = nz // 2
    order_len = args[-1].shape[1]
    vmem = pl.BlockSpec(memory_space=pltpu.VMEM)
    hbm = pl.BlockSpec(memory_space=pl.ANY)
    dma = pltpu.SemaphoreType.DMA
    handed, attended = pl.pallas_call(
        functools.partial(kernel, nz, nsec),
        out_shape=(
            jax.ShapeDtypeStruct((TOK, FEAT), BF16),
            jax.ShapeDtypeStruct((TOK, QH * 128), BF16),
        ),
        in_specs=[hbm] * 12,
        out_specs=(vmem, vmem),
        scratch_shapes=[
            pltpu.VMEM((2, TOK, OWN * 128), BF16),
            pltpu.VMEM((2, TOK, OWN * 128), BF16),
            pltpu.VMEM((2, TOK, 128), BF16),
            pltpu.VMEM((2, TOK, 128), BF16),
            pltpu.VMEM((2, HEADS, TOK), F32),
            pltpu.SMEM((1, HEADS), F32),
            pltpu.SMEM((1, HEADS), F32),
            pltpu.VMEM((1, OWN * 128), F32),
            pltpu.SMEM((1, order_len), jnp.int32),
            pltpu.VMEM((nz, 2, TOK, 128), BF16),
            pltpu.VMEM((2 * QH * TOK, 128), BF16),
            pltpu.VMEM((1, 2 * QH * TOK), F32),
            pltpu.VMEM((1, 2 * QH * TOK), F32),
            pltpu.VMEM((128, 2 * QH * TOK), F32),
            pltpu.VMEM((2, OWN, TOK, 128), F32),
            pltpu.VMEM((2, OWN, TOK + 128, 128), BF16),
            pltpu.VMEM((2, TOK, TOK + 128), BF16),
            pltpu.VMEM((2, OWN, 1, 128), F32),
            pltpu.VMEM((2, OWN, 128, 128), F32),
            pltpu.VMEM((OWN, 1, 128), F32),
            pltpu.VMEM((nz, rows, 128), BF16),
            pltpu.VMEM((nz, rows, 128), BF16),
            pltpu.VMEM((nz, 1, 128), F32),
            pltpu.VMEM((nz, rows, 128), BF16),
            pltpu.VMEM((nz, rows, 128), BF16),
            pltpu.VMEM((2, OWN, TOK, 128), BF16),
            pltpu.VMEM((2, OWN, TOK, 128), BF16),
            pltpu.VMEM((2, 8, 128), F32),
            pltpu.VMEM((2, 8, 128), F32),
            pltpu.VMEM((128, QH * TOK), BF16),
            pltpu.VMEM((128, QH * TOK), BF16),
            pltpu.VMEM((2, 1, QH * TOK), F32),
            pltpu.VMEM((2, 1, QH * TOK), F32),
            dma((2, half + 1, 2)),
            dma((2, half + 1, 2)),
            dma((9,)),
            dma((9,)),
            dma((nz,)),
            dma((nz,)),
            dma((nz,)),
            dma((nz,)),
            dma((nz,)),
            dma((nz,)),
            dma((2 * OWN + 2,)),
            dma((2, OWN + 1)),
            dma((15,)),
        ],
        compiler_params=pltpu.CompilerParams(
            collective_id=0, has_side_effects=True, vmem_limit_bytes=60 * 1024 * 1024
        ),
        cost_estimate=pl.CostEstimate(
            flops=1300000000, bytes_accessed=1400000, transcendentals=2500000
        ),
    )(*flat)
    return handed[None], attended[None]


def solution(mesh):
    nz = mesh.shape["ctx"] // 2
    nsec = mesh.shape["section"]
    wide = P("section", "ctx", "tp")
    return jax.shard_map(
        functools.partial(shards, nz, nsec),
        mesh=mesh,
        in_specs=(
            wide,
            wide,
            wide,
            wide,
            P("section", "tp", "ctx"),
            P("section", "tp"),
            P("section", "tp"),
            P("section", "tp"),
            wide,
            wide,
            wide,
            P("section", None),
        ),
        out_specs=(wide, wide),
        check_vma=False,
    )
```

```python
import functools
import math

import jax
import jax.numpy as jnp
from jax import lax
from jax.experimental import pallas as pl
from jax.experimental.pallas import tpu as pltpu
from jax.sharding import PartitionSpec as P

MESH = pl.DeviceIdType.MESH
F32 = jnp.float32
BF16 = jnp.bfloat16
HIGH = lax.Precision.HIGHEST
NEG = -1e30
TOK = 128
HALF = 64
HEADS = 16
HEADP = 64
FEAT = HEADS * HEADP
TILES = FEAT // 128
OWN = TILES // 2
QH = 4
SCHEDULE = ("h", "h", "lohwh", "whwhw", "")
PIECES = 2
SCALE2 = math.log2(math.e) / math.sqrt(128.0)


def contract(a, b, da, db, precision=None):
    return lax.dot_general(
        a, b, (((da,), (db,)), ((), ())), precision=precision, preferred_element_type=F32
    )


def kernel(
    nz,
    nsec,
    x_in,
    gate_in,
    b_in,
    c_in,
    step_in,
    rate_in,
    skip_in,
    gain_in,
    q_in,
    k_in,
    v_in,
    order_in,
    hand_ref,
    att_ref,
    xs,
    gates,
    writes,
    reads,
    steps,
    rate_ref,
    skip_ref,
    gain_ref,
    order_ref,
    kv,
    qall,
    peak,
    den,
    acc,
    ecum,
    rhs,
    lhs,
    drow,
    cstate,
    dpair,
    pbuf,
    arecv,
    adec,
    pref,
    sin,
    ubuf,
    hrecv,
    sqsend,
    sqrecv,
    osend,
    orecv,
    stsend,
    strecv,
    kv_ss,
    kv_rs,
    y_ss,
    y_rs,
    a_ss,
    a_rs,
    ad_ss,
    ad_rs,
    r_ss,
    r_rs,
    h_ss,
    h_rs,
    in_s,
):
    sec = lax.axis_index("section")
    ctx = lax.axis_index("ctx")
    z = ctx // 2
    y = ctx % 2
    half = nz // 2
    rows = OWN * TOK // nz
    per_tile = TOK // rows
    wide = OWN * 128
    partner = {"ctx": z * 2 + 1 - y}

    def at_z(k):
        return {"ctx": k * 2 + y}

    def around(k):
        return lax.rem(k + nz, nz)

    def in_section(i, t):
        return {"section": lax.rem(sec + i, nsec), "ctx": z * 2 + t}

    def copy(src, dst, ss, rs, to):
        return pltpu.make_async_remote_copy(
            src_ref=src, dst_ref=dst, send_sem=ss, recv_sem=rs, device_id=to, device_id_type=MESH
        )

    sent = []

    def start(c):
        c.start()
        sent.append(c)

    mine = pl.ds(pl.multiple_of(y * wide, 128), wide)

    def theirs(start_at, width):
        return pl.ds(pl.multiple_of((1 - y) * wide + start_at, 128), width)

    fetches = [
        (step_in, steps.at[y]),
        (rate_in, rate_ref),
        (x_in.at[:, mine], xs.at[y]),
        (b_in, writes.at[y]),
        (k_in, kv.at[z, 0:TOK]),
        (v_in, kv.at[z, TOK:]),
        (c_in, reads.at[y]),
        (q_in.at[:, 0:128], qall.at[0:TOK]),
        (q_in.at[:, 128:256], qall.at[TOK : 2 * TOK]),
        (q_in.at[:, 256:384], qall.at[2 * TOK : 3 * TOK]),
        (q_in.at[:, 384:512], qall.at[3 * TOK : 4 * TOK]),
        (order_in, order_ref),
        (gate_in.at[:, mine], gates.at[y]),
        (skip_in, skip_ref),
        (gain_in.at[:, mine], gain_ref),
    ]
    fetches = [pltpu.make_async_copy(s, d, in_s.at[i]) for i, (s, d) in enumerate(fetches)]

    barrier = pltpu.get_barrier_semaphore()
    for o in range(1, nz):
        pl.semaphore_signal(barrier, inc=1, device_id=at_z(around(z + o)), device_id_type=MESH)
    for to in (
        partner,
        in_section(1, 0),
        in_section(1, 1),
        in_section(nsec - 1, 0),
        in_section(nsec - 1, 1),
    ):
        pl.semaphore_signal(barrier, inc=1, device_id=to, device_id_type=MESH)
    for f in fetches:
        f.start()
    pl.semaphore_wait(barrier, nz - 1 + 5)

    hw = wide // 2
    give_steps = copy(step_in, steps.at[y], y_ss.at[0], y_rs.at[0], partner)
    give_b = copy(b_in, writes.at[y], y_ss.at[1], y_rs.at[1], partner)
    give_x = [
        copy(
            x_in.at[:, theirs(i * hw, hw)],
            xs.at[y, :, i * hw : (i + 1) * hw],
            y_ss.at[2 + i],
            y_rs.at[2 + i],
            partner,
        )
        for i in range(2)
    ]
    give_c = copy(c_in, reads.at[y], y_ss.at[4], y_rs.at[4], partner)
    give_gate = copy(gate_in.at[:, theirs(0, wide)], gates.at[y], y_ss.at[5], y_rs.at[5], partner)
    give_q = copy(
        qall.at[pl.ds(0, QH * TOK)], qall.at[pl.ds(QH * TOK, QH * TOK)], y_ss.at[6], y_rs.at[6], partner
    )
    for c in (give_steps, give_b, *give_x):
        start(c)

    piece = 2 * TOK // PIECES

    def ring_copy(way, s, t, arriving):
        if way == 0:
            slot, to = around(z - s + (0 if arriving else 1)), around(z + 1)
        else:
            slot, to = around(z + s - (0 if arriving else 1)), around(z - 1)
        place = kv.at[slot, pl.ds(t * piece, piece)]
        return copy(place, place, kv_ss.at[way, s, t], kv_rs.at[way, s, t], at_z(to))

    def ring_parts(s):
        if s < half:
            return [(w, t) for t in range(PIECES) for w in (0, 1)]
        return [(w, w * PIECES // 2 + t) for t in range(PIECES // 2) for w in (0, 1)]

    def ring_hop(s):
        going = ring_parts(s + 1) if s < half else []
        for w, t in ring_parts(s):
            ring_copy(w, s, t, True).wait_recv()
            if (w, t) in going:
                start(ring_copy(w, s + 1, t, False))

    hops = iter(range(1, half + 1))
    parts = iter(range(1, half + 1))

    def run(what):
        for item in what:
            if item == "o":
                give_q.wait_recv()
                attend([z], first=True)
            elif item == "l":
                give_c.wait_recv()
                block_lhs(0)
                block_lhs(1)
            else:
                s = next(hops if item == "h" else parts, None)
                if s is not None:
                    (ring_hop if item == "h" else attend_step)(s)

    for f in fetches[:6]:
        f.wait()
    for w, t in ring_parts(1):
        start(ring_copy(w, 1, t, False))
    row16 = lax.broadcasted_iota(jnp.int32, (HEADS, TOK), 0)
    rate = jnp.zeros((HEADS, TOK), F32)
    for h in range(HEADS):
        rate = jnp.where(row16 == h, rate_ref[0, h], rate)
    row = lax.broadcasted_iota(jnp.int32, (TOK, 128), 0)
    lane = lax.broadcasted_iota(jnp.int32, (TOK, 128), 1)
    upper = jnp.where(row <= lane, 1.0, 0.0).astype(F32)
    lane_head = lax.shift_right_logical(lane[:HEADS], 6)

    def spread_of(c):
        return jnp.where(row16 - y * (2 * OWN) - 2 * c == lane_head, 1.0, 0.0).astype(F32)

    def scales_of(t):
        step = steps[t]
        cum = contract(-rate * step, upper, 1, 0, HIGH)
        return jnp.concatenate([jnp.exp(cum), jnp.exp(-cum) * step], axis=1)

    def block_tile(t, scales, c, t_is_mine):
        cols = slice(c * 128, (c + 1) * 128)
        spread_out = contract(scales, spread_of(c), 0, 0, HIGH)
        ecum[t, c] = spread_out[:TOK]
        d = spread_out[TOK - 1 : TOK]
        if t_is_mine:
            drow[t, c] = d
        xf = (xs[t, :, cols].astype(F32) * spread_out[TOK:]).astype(BF16)
        rhs[t, c, 0:TOK] = xf
        cstate[t, c] = contract(writes[t], xf, 0, 0) * d

    def block_lhs(t):
        inner = contract(reads[t], writes[t], 1, 1)
        lhs[t, :, 0:TOK] = jnp.where(lane <= row, inner, 0.0).astype(BF16)
        lhs[t, :, TOK:] = reads[t]

    scales = scales_of(y)
    for c in range(OWN):
        block_tile(y, scales, c, True)
    far_first = sorted(range(1, nz), key=lambda o: -min(o, nz - o))
    for f in fetches[6:]:
        f.wait()
    run(SCHEDULE[0])
    give_steps.wait_recv()
    scales = scales_of(1 - y)
    for c in range(OWN):
        d = contract(scales[:, TOK - 8 : TOK], spread_of(c), 0, 0, HIGH)[7:8]
        drow[1 - y, c] = d
        dpair[c] = drow[y, c] * d
    for o in far_first:
        k = around(z + o)
        start(copy(dpair.at[k // per_tile], adec.at[z], ad_ss.at[o], ad_rs.at[z], at_z(k)))
    adec[z] = dpair[z // per_tile]
    start(give_c)
    start(give_q)
    start(give_gate)
    run(SCHEDULE[1])
    give_b.wait_recv()
    for c in range(OWN):
        if c % (OWN // 2) == 0:
            give_x[c // (OWN // 2)].wait_recv()
        block_tile(1 - y, scales, c, False)
        total = cstate[0, c] * drow[1, c] + cstate[1, c]
        for r in range(per_tile):
            pbuf[c * per_tile + r] = total[r * rows : (r + 1) * rows].astype(BF16)
    for o in far_first:
        k = around(z + o)
        start(copy(pbuf.at[k], arecv.at[z], a_ss.at[o], a_rs.at[z], at_z(k)))
    arecv[z] = pbuf[z]

    row_in = jnp.bitwise_and(row, HALF - 1)
    lane1 = lax.broadcasted_iota(jnp.int32, (1, 128), 1)

    def query_pos(at):
        o0 = order_ref[0, 2 * at]
        o1 = order_ref[0, 2 * at + 1]
        return jnp.where(lane1 < HALF, o0, o1) * HALF + jnp.bitwise_and(lane1, HALF - 1)

    qpos = [query_pos(ctx), query_pos(z * 2 + 1 - y)]

    def attend(slots, first=False, after_partner=None):
        biases = []
        for slot in slots:
            at = slot * 2 + y
            o0 = order_ref[0, 2 * at]
            o1 = order_ref[0, 2 * at + 1]
            kpos = jnp.where(row < HALF, o0, o1) * HALF + row_in
            biases.append([jnp.where(kpos <= p, 0.0, NEG).astype(F32) for p in qpos])
        keys = jnp.concatenate([kv[s, 0:TOK] for s in slots], axis=0)
        values = jnp.concatenate([kv[s, TOK:] for s in slots], axis=0)
        for src in (1, 0):
            bias = jnp.concatenate([b[src] for b in biases], axis=0)
            bias = jnp.concatenate([bias, bias], axis=1)
            for pair in range(QH // 2):
                cols = slice(src * QH * TOK + pair * 256, src * QH * TOK + (pair + 1) * 256)
                scores = contract(keys, qall[cols], 1, 1) + bias
                new = jnp.max(scores, axis=0, keepdims=True)
                if not first:
                    old = peak[:, cols]
                    new = jnp.maximum(old, new)
                weights = jnp.exp2((scores - new) * SCALE2)
                total = jnp.sum(weights, axis=0, keepdims=True)
                summed = contract(values, weights.astype(BF16), 0, 0)
                if not first:
                    fade = jnp.exp2((old - new) * SCALE2)
                    total += den[:, cols] * fade
                    summed += acc[:, cols] * fade
                peak[:, cols] = new
                den[:, cols] = total
                acc[:, cols] = summed
            if src == 1 and after_partner is not None:
                after_partner()

    def partial_copies():
        return [copy(stsend, strecv, y_ss.at[7], y_rs.at[7], partner)] + [
            copy(osend.at[h], orecv.at[h], y_ss.at[8 + h], y_rs.at[8 + h], partner)
            for h in range(QH)
        ]

    def give_partial():
        copies = partial_copies()
        other_cols = slice(QH * TOK, 2 * QH * TOK)
        stsend[0] = peak[:, other_cols]
        stsend[1] = den[:, other_cols]
        start(copies[0])
        for h in range(QH):
            cols = slice((QH + h) * TOK, (QH + h + 1) * TOK)
            osend[h] = (acc[:, cols] / den[:, cols]).astype(BF16)
            start(copies[1 + h])

    def attend_step(s):
        if s < half:
            attend([around(z - s), around(z + s)])
        else:
            attend([around(z - s)], after_partner=give_partial)

    run(SCHEDULE[2])

    for o in range(1, nz):
        k = around(z + o)
        copy(dpair.at[0], adec.at[k], ad_ss.at[o], ad_rs.at[k], at_z(k)).wait_recv()
        copy(pbuf.at[k], arecv.at[k], a_ss.at[o], a_rs.at[k], at_z(k)).wait_recv()
    state = jnp.zeros((rows, 128), F32)
    for k in range(nz):
        pref[k] = state.astype(BF16)
        state = adec[k] * state + arecv[k].astype(F32)
    for o in far_first:
        k = around(z + o)
        start(copy(pref.at[k], sin.at[z], r_ss.at[o], r_rs.at[z], at_z(k)))
    sin[z] = pref[z]

    run(SCHEDULE[3])
    give_gate.wait_recv()

    for o in range(1, nz):
        k = around(z + o)
        copy(pref.at[k], sin.at[k], r_ss.at[o], r_rs.at[k], at_z(k)).wait_recv()
    squares = [jnp.zeros((TOK, 128), F32) for _ in range(2)]
    for c in range(OWN):
        cols = slice(c * 128, (c + 1) * 128)
        enter = jnp.concatenate([sin[c * per_tile + r] for r in range(per_tile)], axis=0)
        rhs[0, c, TOK:] = enter
        rhs[1, c, TOK:] = (drow[0, c] * enter.astype(F32) + cstate[0, c]).astype(BF16)
        at = y * (2 * OWN) + 2 * c
        skip = jnp.where(lane1 < HEADP, skip_ref[0, at], skip_ref[0, at + 1])
        for t in range(2):
            out = ecum[t, c] * contract(lhs[t], rhs[t, c], 1, 0)
            out += skip * xs[t, :, cols].astype(F32)
            gate = gates[t, :, cols].astype(F32)
            value = out * (gate / (1.0 + jnp.exp(-gate)))
            squares[t] += value * value
            ubuf[t, c] = (value * gain_ref[:, cols]).astype(BF16)
            i = t * OWN + c
            start(copy(ubuf.at[t, c], hrecv.at[y, c], h_ss.at[i], h_rs.at[y, c], in_section(1, t)))
    ones = jnp.ones((8, 128), F32)
    for t in range(2):
        sqsend[t] = contract(ones, squares[t], 1, 1, HIGH)
        i = 2 * OWN + t
        start(copy(sqsend.at[t], sqrecv.at[y], h_ss.at[i], h_rs.at[y, OWN], in_section(1, t)))

    run(SCHEDULE[4] + "hw" * half)

    for u in range(2):
        for c in range(OWN):
            copy(ubuf.at[0, c], hrecv.at[u, c], h_ss.at[c], h_rs.at[u, c], partner).wait_recv()
        copy(sqsend.at[0], sqrecv.at[u], h_ss.at[2 * OWN], h_rs.at[u, OWN], partner).wait_recv()
    factor = lax.rsqrt((sqrecv[0] + sqrecv[1]) * (1.0 / FEAT) + 1e-5)
    pick = jnp.where(row[:8] == 0, 1.0, 0.0).astype(F32)
    factor = contract(factor, pick, 0, 0, HIGH)
    for u in range(2):
        for c in range(OWN):
            j = u * OWN + c
            hand_ref[:, j * 128 : (j + 1) * 128] = (hrecv[u, c].astype(F32) * factor).astype(BF16)

    swaps = partial_copies()
    swaps[0].wait_recv()
    mine_cols = slice(0, QH * TOK)
    m1 = peak[:, mine_cols]
    m2 = strecv[0]
    top = jnp.maximum(m1, m2)
    w1 = jnp.exp2((m1 - top) * SCALE2)
    w2 = jnp.exp2((m2 - top) * SCALE2) * strecv[1]
    inv = 1.0 / (w1 * den[:, mine_cols] + w2)
    w1 = w1 * inv
    w2 = w2 * inv
    for h in range(QH):
        cols = slice(h * TOK, (h + 1) * TOK)
        swaps[1 + h].wait_recv()
        both = acc[:, cols] * w1[:, cols] + orecv[h].astype(F32) * w2[:, cols]
        att_ref[:, cols] = both.T.astype(BF16)

    for c in sent:
        c.wait_send()


def deliver(half_rows, hand_in, att_in, hand_out, att_out, sems):
    copies = []
    for i, (src, dst) in enumerate(((hand_in, hand_out), (att_in, att_out))):
        for p in range(2):
            part = pl.ds(p * half_rows, half_rows)
            copies.append(pltpu.make_async_copy(src.at[part], dst.at[part], sems.at[2 * i + p]))
    for c in copies:
        c.start()
    for c in copies:
        c.wait()


def shards(nz, nsec, *args):
    flat = [a.reshape(a.shape[1:]) if a.ndim == 3 else a for a in args]
    rows = OWN * TOK // nz
    half = nz // 2
    order_len = args[-1].shape[1]
    vmem = pl.BlockSpec(memory_space=pltpu.VMEM)
    hbm = pl.BlockSpec(memory_space=pl.ANY)
    dma = pltpu.SemaphoreType.DMA
    handed, attended = pl.pallas_call(
        functools.partial(kernel, nz, nsec),
        out_shape=(
            jax.ShapeDtypeStruct((TOK, FEAT), BF16),
            jax.ShapeDtypeStruct((TOK, QH * 128), BF16),
        ),
        in_specs=[hbm] * 12,
        out_specs=(vmem, vmem),
        scratch_shapes=[
            pltpu.VMEM((2, TOK, OWN * 128), BF16),
            pltpu.VMEM((2, TOK, OWN * 128), BF16),
            pltpu.VMEM((2, TOK, 128), BF16),
            pltpu.VMEM((2, TOK, 128), BF16),
            pltpu.VMEM((2, HEADS, TOK), F32),
            pltpu.SMEM((1, HEADS), F32),
            pltpu.SMEM((1, HEADS), F32),
            pltpu.VMEM((1, OWN * 128), F32),
            pltpu.SMEM((1, order_len), jnp.int32),
            pltpu.VMEM((nz, 2 * TOK, 128), BF16),
            pltpu.VMEM((2 * QH * TOK, 128), BF16),
            pltpu.VMEM((1, 2 * QH * TOK), F32),
            pltpu.VMEM((1, 2 * QH * TOK), F32),
            pltpu.VMEM((128, 2 * QH * TOK), F32),
            pltpu.VMEM((2, OWN, TOK, 128), F32),
            pltpu.VMEM((2, OWN, TOK + 128, 128), BF16),
            pltpu.VMEM((2, TOK, TOK + 128), BF16),
            pltpu.VMEM((2, OWN, 1, 128), F32),
            pltpu.VMEM((2, OWN, 128, 128), F32),
            pltpu.VMEM((OWN, 1, 128), F32),
            pltpu.VMEM((nz, rows, 128), BF16),
            pltpu.VMEM((nz, rows, 128), BF16),
            pltpu.VMEM((nz, 1, 128), F32),
            pltpu.VMEM((nz, rows, 128), BF16),
            pltpu.VMEM((nz, rows, 128), BF16),
            pltpu.VMEM((2, OWN, TOK, 128), BF16),
            pltpu.VMEM((2, OWN, TOK, 128), BF16),
            pltpu.VMEM((2, 8, 128), F32),
            pltpu.VMEM((2, 8, 128), F32),
            pltpu.VMEM((QH, 128, TOK), BF16),
            pltpu.VMEM((QH, 128, TOK), BF16),
            pltpu.VMEM((2, 1, QH * TOK), F32),
            pltpu.VMEM((2, 1, QH * TOK), F32),
            dma((2, half + 1, PIECES)),
            dma((2, half + 1, PIECES)),
            dma((8 + QH,)),
            dma((8 + QH,)),
            dma((nz,)),
            dma((nz,)),
            dma((nz,)),
            dma((nz,)),
            dma((nz,)),
            dma((nz,)),
            dma((2 * OWN + 2,)),
            dma((2, OWN + 1)),
            dma((15,)),
        ],
        compiler_params=pltpu.CompilerParams(
            collective_id=0, has_side_effects=True, vmem_limit_bytes=60 * 1024 * 1024
        ),
        cost_estimate=pl.CostEstimate(
            flops=1300000000, bytes_accessed=1400000, transcendentals=2500000
        ),
    )(*flat)
    half_rows = TOK // 2
    handed, attended = pl.pallas_call(
        functools.partial(deliver, half_rows),
        out_shape=(
            jax.ShapeDtypeStruct((TOK, FEAT), BF16),
            jax.ShapeDtypeStruct((TOK, QH * 128), BF16),
        ),
        in_specs=[hbm, hbm],
        out_specs=(hbm, hbm),
        scratch_shapes=[dma((4,))],
    )(handed, attended)
    return handed[None], attended[None]


def solution(mesh):
    nz = mesh.shape["ctx"] // 2
    nsec = mesh.shape["section"]
    wide = P("section", "ctx", "tp")
    return jax.shard_map(
        functools.partial(shards, nz, nsec),
        mesh=mesh,
        in_specs=(
            wide,
            wide,
            wide,
            wide,
            P("section", "tp", "ctx"),
            P("section", "tp"),
            P("section", "tp"),
            P("section", "tp"),
            wide,
            wide,
            wide,
            P("section", None),
        ),
        out_specs=(wide, wide),
        check_vma=False,
    )
```

```python
import functools
import math

import jax
import jax.numpy as jnp
from jax import lax
from jax.experimental import pallas as pl
from jax.experimental.pallas import tpu as pltpu
from jax.sharding import PartitionSpec as P

MESH = pl.DeviceIdType.MESH
F32 = jnp.float32
BF16 = jnp.bfloat16
HIGH = lax.Precision.HIGHEST
NEG = -1e30
TOK = 128
HALF = 64
HEADS = 16
HEADP = 64
FEAT = HEADS * HEADP
TILES = FEAT // 128
OWN = TILES // 2
QH = 4
SCHEDULE = ("h", "h", "lohwh", "whwhw", "")
PIECES = 2
SCALE2 = math.log2(math.e) / math.sqrt(128.0)


def contract(a, b, da, db, precision=None):
    return lax.dot_general(
        a, b, (((da,), (db,)), ((), ())), precision=precision, preferred_element_type=F32
    )


def kernel(
    nz,
    nsec,
    x_in,
    gate_in,
    b_in,
    c_in,
    step_in,
    rate_in,
    skip_in,
    gain_in,
    q_in,
    k_in,
    v_in,
    order_in,
    hand_ref,
    att_ref,
    xs,
    gates,
    writes,
    reads,
    steps,
    rate_ref,
    skip_ref,
    gain_ref,
    order_ref,
    kv,
    qall,
    peak,
    den,
    acc,
    ecum,
    rhs,
    lhs,
    drow,
    cstate,
    dpair,
    pbuf,
    arecv,
    adec,
    pref,
    sin,
    ubuf,
    hrecv,
    sqsend,
    sqrecv,
    osend,
    orecv,
    stsend,
    strecv,
    kv_ss,
    kv_rs,
    y_ss,
    y_rs,
    a_ss,
    a_rs,
    ad_ss,
    ad_rs,
    r_ss,
    r_rs,
    h_ss,
    h_rs,
    in_s,
):
    sec = lax.axis_index("section")
    ctx = lax.axis_index("ctx")
    z = ctx // 2
    y = ctx % 2
    half = nz // 2
    rows = OWN * TOK // nz
    per_tile = TOK // rows
    wide = OWN * 128
    partner = {"ctx": z * 2 + 1 - y}

    def at_z(k):
        return {"ctx": k * 2 + y}

    def around(k):
        return lax.rem(k + nz, nz)

    def in_section(i, t):
        return {"section": lax.rem(sec + i, nsec), "ctx": z * 2 + t}

    def copy(src, dst, ss, rs, to):
        return pltpu.make_async_remote_copy(
            src_ref=src, dst_ref=dst, send_sem=ss, recv_sem=rs, device_id=to, device_id_type=MESH
        )

    sent = []

    def start(c):
        c.start()
        sent.append(c)

    mine = pl.ds(pl.multiple_of(y * wide, 128), wide)

    def theirs(start_at, width):
        return pl.ds(pl.multiple_of((1 - y) * wide + start_at, 128), width)

    fetches = [
        (step_in, steps.at[y]),
        (rate_in, rate_ref),
        (x_in.at[:, mine], xs.at[y]),
        (b_in, writes.at[y]),
        (k_in, kv.at[z, 0:TOK]),
        (v_in, kv.at[z, TOK:]),
        (c_in, reads.at[y]),
        (q_in.at[:, 0:128], qall.at[0:TOK]),
        (q_in.at[:, 128:256], qall.at[TOK : 2 * TOK]),
        (q_in.at[:, 256:384], qall.at[2 * TOK : 3 * TOK]),
        (q_in.at[:, 384:512], qall.at[3 * TOK : 4 * TOK]),
        (order_in, order_ref),
        (gate_in.at[:, mine], gates.at[y]),
        (skip_in, skip_ref),
        (gain_in.at[:, mine], gain_ref),
    ]
    fetches = [pltpu.make_async_copy(s, d, in_s.at[i]) for i, (s, d) in enumerate(fetches)]

    barrier = pltpu.get_barrier_semaphore()
    for o in range(1, nz):
        pl.semaphore_signal(barrier, inc=1, device_id=at_z(around(z + o)), device_id_type=MESH)
    for to in (
        partner,
        in_section(1, 0),
        in_section(1, 1),
        in_section(nsec - 1, 0),
        in_section(nsec - 1, 1),
    ):
        pl.semaphore_signal(barrier, inc=1, device_id=to, device_id_type=MESH)
    for f in fetches:
        f.start()
    pl.semaphore_wait(barrier, nz - 1 + 5)

    hw = wide // 2
    give_steps = copy(step_in, steps.at[y], y_ss.at[0], y_rs.at[0], partner)
    give_b = copy(b_in, writes.at[y], y_ss.at[1], y_rs.at[1], partner)
    give_x = [
        copy(
            x_in.at[:, theirs(i * hw, hw)],
            xs.at[y, :, i * hw : (i + 1) * hw],
            y_ss.at[2 + i],
            y_rs.at[2 + i],
            partner,
        )
        for i in range(2)
    ]
    give_c = copy(c_in, reads.at[y], y_ss.at[4], y_rs.at[4], partner)
    give_gate = copy(gate_in.at[:, theirs(0, wide)], gates.at[y], y_ss.at[5], y_rs.at[5], partner)
    give_q = copy(
        qall.at[pl.ds(0, QH * TOK)], qall.at[pl.ds(QH * TOK, QH * TOK)], y_ss.at[6], y_rs.at[6], partner
    )
    for c in (give_steps, give_b, *give_x):
        start(c)

    piece = 2 * TOK // PIECES

    def ring_copy(way, s, t, arriving):
        if way == 0:
            slot, to = around(z - s + (0 if arriving else 1)), around(z + 1)
        else:
            slot, to = around(z + s - (0 if arriving else 1)), around(z - 1)
        place = kv.at[slot, pl.ds(t * piece, piece)]
        return copy(place, place, kv_ss.at[way, s, t], kv_rs.at[way, s, t], at_z(to))

    def ring_parts(s):
        if s < half:
            return [(w, t) for t in range(PIECES) for w in (0, 1)]
        return [(w, w * PIECES // 2 + t) for t in range(PIECES // 2) for w in (0, 1)]

    def ring_hop(s):
        going = ring_parts(s + 1) if s < half else []
        for w, t in ring_parts(s):
            ring_copy(w, s, t, True).wait_recv()
            if (w, t) in going:
                start(ring_copy(w, s + 1, t, False))

    hops = iter(range(1, half + 1))
    parts = iter(range(1, half + 1))

    def run(what):
        for item in what:
            if item == "o":
                give_q.wait_recv()
                attend([z], first=True)
            elif item == "l":
                give_c.wait_recv()
                block_lhs(0)
                block_lhs(1)
            else:
                s = next(hops if item == "h" else parts, None)
                if s is not None:
                    (ring_hop if item == "h" else attend_step)(s)

    for f in fetches[:6]:
        f.wait()
    for w, t in ring_parts(1):
        start(ring_copy(w, 1, t, False))
    row16 = lax.broadcasted_iota(jnp.int32, (HEADS, TOK), 0)
    rate = jnp.zeros((HEADS, TOK), F32)
    for h in range(HEADS):
        rate = jnp.where(row16 == h, rate_ref[0, h], rate)
    row = lax.broadcasted_iota(jnp.int32, (TOK, 128), 0)
    lane = lax.broadcasted_iota(jnp.int32, (TOK, 128), 1)
    upper = jnp.where(row <= lane, 1.0, 0.0).astype(F32)
    lane_head = lax.shift_right_logical(lane[:HEADS], 6)

    def spread_of(c):
        one = jnp.where(row16 - y * (2 * OWN) - 2 * c == lane_head, 1.0, 0.0).astype(BF16)
        return jnp.concatenate([one] * 3, axis=0)

    def scales_of(t):
        step = steps[t]
        cum = contract(-rate * step, upper, 1, 0, HIGH)
        whole = jnp.concatenate([jnp.exp(cum), jnp.exp(-cum) * step], axis=1)
        high = whole.astype(BF16)
        rest = whole - high.astype(F32)
        middle = rest.astype(BF16)
        low = (rest - middle.astype(F32)).astype(BF16)
        return jnp.concatenate([high, middle, low], axis=0)

    def block_tile(t, scales, c, t_is_mine):
        cols = slice(c * 128, (c + 1) * 128)
        spread_out = contract(scales, spread_of(c), 0, 0)
        ecum[t, c] = spread_out[:TOK]
        d = spread_out[TOK - 1 : TOK]
        if t_is_mine:
            drow[t, c] = d
        xf = (xs[t, :, cols].astype(F32) * spread_out[TOK:]).astype(BF16)
        rhs[t, c, 0:TOK] = xf
        cstate[t, c] = contract(writes[t], xf, 0, 0) * d

    def block_lhs(t):
        inner = contract(reads[t], writes[t], 1, 1)
        lhs[t, :, 0:TOK] = jnp.where(lane <= row, inner, 0.0).astype(BF16)
        lhs[t, :, TOK:] = reads[t]

    scales = scales_of(y)
    for c in range(OWN):
        block_tile(y, scales, c, True)
    far_first = sorted(range(1, nz), key=lambda o: -min(o, nz - o))
    for f in fetches[6:]:
        f.wait()
    run(SCHEDULE[0])
    give_steps.wait_recv()
    scales = scales_of(1 - y)
    for c in range(OWN):
        d = contract(scales[:, 0:TOK], spread_of(c), 0, 0)[TOK - 1 : TOK]
        drow[1 - y, c] = d
        dpair[c] = drow[y, c] * d
    for o in far_first:
        k = around(z + o)
        start(copy(dpair.at[k // per_tile], adec.at[z], ad_ss.at[o], ad_rs.at[z], at_z(k)))
    adec[z] = dpair[z // per_tile]
    start(give_c)
    start(give_q)
    start(give_gate)
    run(SCHEDULE[1])
    give_b.wait_recv()
    for c in range(OWN):
        if c % (OWN // 2) == 0:
            give_x[c // (OWN // 2)].wait_recv()
        block_tile(1 - y, scales, c, False)
        total = cstate[0, c] * drow[1, c] + cstate[1, c]
        for r in range(per_tile):
            pbuf[c * per_tile + r] = total[r * rows : (r + 1) * rows].astype(BF16)
    for o in far_first:
        k = around(z + o)
        start(copy(pbuf.at[k], arecv.at[z], a_ss.at[o], a_rs.at[z], at_z(k)))
    arecv[z] = pbuf[z]

    row_in = jnp.bitwise_and(row, HALF - 1)
    lane1 = lax.broadcasted_iota(jnp.int32, (1, 128), 1)

    def query_pos(at):
        o0 = order_ref[0, 2 * at]
        o1 = order_ref[0, 2 * at + 1]
        return jnp.where(lane1 < HALF, o0, o1) * HALF + jnp.bitwise_and(lane1, HALF - 1)

    qpos = [query_pos(ctx), query_pos(z * 2 + 1 - y)]

    def attend(slots, first=False, after_partner=None):
        biases = []
        for slot in slots:
            at = slot * 2 + y
            o0 = order_ref[0, 2 * at]
            o1 = order_ref[0, 2 * at + 1]
            kpos = jnp.where(row < HALF, o0, o1) * HALF + row_in
            biases.append([jnp.where(kpos <= p, 0.0, NEG).astype(F32) for p in qpos])
        keys = jnp.concatenate([kv[s, 0:TOK] for s in slots], axis=0)
        values = jnp.concatenate([kv[s, TOK:] for s in slots], axis=0)
        for src in (1, 0):
            bias = jnp.concatenate([b[src] for b in biases], axis=0)
            bias = jnp.concatenate([bias, bias], axis=1)
            for pair in range(QH // 2):
                cols = slice(src * QH * TOK + pair * 256, src * QH * TOK + (pair + 1) * 256)
                scores = contract(keys, qall[cols], 1, 1) + bias
                new = jnp.max(scores, axis=0, keepdims=True)
                if not first:
                    old = peak[:, cols]
                    new = jnp.maximum(old, new)
                weights = jnp.exp2((scores - new) * SCALE2)
                total = jnp.sum(weights, axis=0, keepdims=True)
                summed = contract(values, weights.astype(BF16), 0, 0)
                if not first:
                    fade = jnp.exp2((old - new) * SCALE2)
                    total += den[:, cols] * fade
                    summed += acc[:, cols] * fade
                peak[:, cols] = new
                den[:, cols] = total
                acc[:, cols] = summed
            if src == 1 and after_partner is not None:
                after_partner()

    def partial_copies():
        return [copy(stsend, strecv, y_ss.at[7], y_rs.at[7], partner)] + [
            copy(osend.at[h], orecv.at[h], y_ss.at[8 + h], y_rs.at[8 + h], partner)
            for h in range(QH)
        ]

    def give_partial():
        copies = partial_copies()
        other_cols = slice(QH * TOK, 2 * QH * TOK)
        stsend[0] = peak[:, other_cols]
        stsend[1] = den[:, other_cols]
        start(copies[0])
        for h in range(QH):
            cols = slice((QH + h) * TOK, (QH + h + 1) * TOK)
            osend[h] = (acc[:, cols] / den[:, cols]).astype(BF16)
            start(copies[1 + h])

    def attend_step(s):
        if s < half:
            attend([around(z - s), around(z + s)])
        else:
            attend([around(z - s)], after_partner=give_partial)

    run(SCHEDULE[2])

    for o in range(1, nz):
        k = around(z + o)
        copy(dpair.at[0], adec.at[k], ad_ss.at[o], ad_rs.at[k], at_z(k)).wait_recv()
        copy(pbuf.at[k], arecv.at[k], a_ss.at[o], a_rs.at[k], at_z(k)).wait_recv()
    state = jnp.zeros((rows, 128), F32)
    for k in range(nz):
        pref[k] = state.astype(BF16)
        state = adec[k] * state + arecv[k].astype(F32)
    for o in far_first:
        k = around(z + o)
        start(copy(pref.at[k], sin.at[z], r_ss.at[o], r_rs.at[z], at_z(k)))
    sin[z] = pref[z]

    run(SCHEDULE[3])
    give_gate.wait_recv()

    for o in range(1, nz):
        k = around(z + o)
        copy(pref.at[k], sin.at[k], r_ss.at[o], r_rs.at[k], at_z(k)).wait_recv()
    squares = [jnp.zeros((TOK, 128), F32) for _ in range(2)]
    for c in range(OWN):
        cols = slice(c * 128, (c + 1) * 128)
        enter = jnp.concatenate([sin[c * per_tile + r] for r in range(per_tile)], axis=0)
        rhs[0, c, TOK:] = enter
        rhs[1, c, TOK:] = (drow[0, c] * enter.astype(F32) + cstate[0, c]).astype(BF16)
        at = y * (2 * OWN) + 2 * c
        skip = jnp.where(lane1 < HEADP, skip_ref[0, at], skip_ref[0, at + 1])
        for t in range(2):
            out = ecum[t, c] * contract(lhs[t], rhs[t, c], 1, 0)
            out += skip * xs[t, :, cols].astype(F32)
            gate = gates[t, :, cols].astype(F32)
            value = out * (gate / (1.0 + jnp.exp(-gate)))
            squares[t] += value * value
            ubuf[t, c] = (value * gain_ref[:, cols]).astype(BF16)
            i = t * OWN + c
            start(copy(ubuf.at[t, c], hrecv.at[y, c], h_ss.at[i], h_rs.at[y, c], in_section(1, t)))
    ones = jnp.ones((8, 128), F32)
    for t in range(2):
        sqsend[t] = contract(ones, squares[t], 1, 1, HIGH)
        i = 2 * OWN + t
        start(copy(sqsend.at[t], sqrecv.at[y], h_ss.at[i], h_rs.at[y, OWN], in_section(1, t)))

    run(SCHEDULE[4] + "hw" * half)

    for u in range(2):
        for c in range(OWN):
            copy(ubuf.at[0, c], hrecv.at[u, c], h_ss.at[c], h_rs.at[u, c], partner).wait_recv()
        copy(sqsend.at[0], sqrecv.at[u], h_ss.at[2 * OWN], h_rs.at[u, OWN], partner).wait_recv()
    factor = lax.rsqrt((sqrecv[0] + sqrecv[1]) * (1.0 / FEAT) + 1e-5)
    pick = jnp.where(row[:8] == 0, 1.0, 0.0).astype(F32)
    factor = contract(factor, pick, 0, 0, HIGH)
    for u in range(2):
        for c in range(OWN):
            j = u * OWN + c
            hand_ref[:, j * 128 : (j + 1) * 128] = (hrecv[u, c].astype(F32) * factor).astype(BF16)

    swaps = partial_copies()
    swaps[0].wait_recv()
    mine_cols = slice(0, QH * TOK)
    m1 = peak[:, mine_cols]
    m2 = strecv[0]
    top = jnp.maximum(m1, m2)
    w1 = jnp.exp2((m1 - top) * SCALE2)
    w2 = jnp.exp2((m2 - top) * SCALE2) * strecv[1]
    inv = 1.0 / (w1 * den[:, mine_cols] + w2)
    w1 = w1 * inv
    w2 = w2 * inv
    for h in range(QH):
        cols = slice(h * TOK, (h + 1) * TOK)
        swaps[1 + h].wait_recv()
        both = acc[:, cols] * w1[:, cols] + orecv[h].astype(F32) * w2[:, cols]
        att_ref[:, cols] = both.T.astype(BF16)

    for c in sent:
        c.wait_send()


def deliver(hand_in, att_in, hand_out, att_out):
    hand_out[...] = hand_in[...]
    att_out[...] = att_in[...]


def shards(nz, nsec, *args):
    flat = [a.reshape(a.shape[1:]) if a.ndim == 3 else a for a in args]
    rows = OWN * TOK // nz
    half = nz // 2
    order_len = args[-1].shape[1]
    vmem = pl.BlockSpec(memory_space=pltpu.VMEM)
    hbm = pl.BlockSpec(memory_space=pl.ANY)
    dma = pltpu.SemaphoreType.DMA
    handed, attended = pl.pallas_call(
        functools.partial(kernel, nz, nsec),
        out_shape=(
            jax.ShapeDtypeStruct((TOK, FEAT), BF16),
            jax.ShapeDtypeStruct((TOK, QH * 128), BF16),
        ),
        in_specs=[hbm] * 12,
        out_specs=(vmem, vmem),
        scratch_shapes=[
            pltpu.VMEM((2, TOK, OWN * 128), BF16),
            pltpu.VMEM((2, TOK, OWN * 128), BF16),
            pltpu.VMEM((2, TOK, 128), BF16),
            pltpu.VMEM((2, TOK, 128), BF16),
            pltpu.VMEM((2, HEADS, TOK), F32),
            pltpu.SMEM((1, HEADS), F32),
            pltpu.SMEM((1, HEADS), F32),
            pltpu.VMEM((1, OWN * 128), F32),
            pltpu.SMEM((1, order_len), jnp.int32),
            pltpu.VMEM((nz, 2 * TOK, 128), BF16),
            pltpu.VMEM((2 * QH * TOK, 128), BF16),
            pltpu.VMEM((1, 2 * QH * TOK), F32),
            pltpu.VMEM((1, 2 * QH * TOK), F32),
            pltpu.VMEM((128, 2 * QH * TOK), F32),
            pltpu.VMEM((2, OWN, TOK, 128), F32),
            pltpu.VMEM((2, OWN, TOK + 128, 128), BF16),
            pltpu.VMEM((2, TOK, TOK + 128), BF16),
            pltpu.VMEM((2, OWN, 1, 128), F32),
            pltpu.VMEM((2, OWN, 128, 128), F32),
            pltpu.VMEM((OWN, 1, 128), F32),
            pltpu.VMEM((nz, rows, 128), BF16),
            pltpu.VMEM((nz, rows, 128), BF16),
            pltpu.VMEM((nz, 1, 128), F32),
            pltpu.VMEM((nz, rows, 128), BF16),
            pltpu.VMEM((nz, rows, 128), BF16),
            pltpu.VMEM((2, OWN, TOK, 128), BF16),
            pltpu.VMEM((2, OWN, TOK, 128), BF16),
            pltpu.VMEM((2, 8, 128), F32),
            pltpu.VMEM((2, 8, 128), F32),
            pltpu.VMEM((QH, 128, TOK), BF16),
            pltpu.VMEM((QH, 128, TOK), BF16),
            pltpu.VMEM((2, 1, QH * TOK), F32),
            pltpu.VMEM((2, 1, QH * TOK), F32),
            dma((2, half + 1, PIECES)),
            dma((2, half + 1, PIECES)),
            dma((8 + QH,)),
            dma((8 + QH,)),
            dma((nz,)),
            dma((nz,)),
            dma((nz,)),
            dma((nz,)),
            dma((nz,)),
            dma((nz,)),
            dma((2 * OWN + 2,)),
            dma((2, OWN + 1)),
            dma((15,)),
        ],
        compiler_params=pltpu.CompilerParams(
            collective_id=0, has_side_effects=True, vmem_limit_bytes=60 * 1024 * 1024
        ),
        cost_estimate=pl.CostEstimate(
            flops=1300000000, bytes_accessed=1400000, transcendentals=2500000
        ),
    )(*flat)
    handed, attended = pl.pallas_call(
        deliver,
        out_shape=(
            jax.ShapeDtypeStruct((TOK, FEAT), BF16),
            jax.ShapeDtypeStruct((TOK, QH * 128), BF16),
        ),
        in_specs=[vmem, vmem],
        out_specs=(vmem, vmem),
    )(handed, attended)
    return handed[None], attended[None]


def solution(mesh):
    nz = mesh.shape["ctx"] // 2
    nsec = mesh.shape["section"]
    wide = P("section", "ctx", "tp")
    return jax.shard_map(
        functools.partial(shards, nz, nsec),
        mesh=mesh,
        in_specs=(
            wide,
            wide,
            wide,
            wide,
            P("section", "tp", "ctx"),
            P("section", "tp"),
            P("section", "tp"),
            P("section", "tp"),
            wide,
            wide,
            wide,
            P("section", None),
        ),
        out_specs=(wide, wide),
        check_vma=False,
    )
```
